256 devices in a mesh: query: 16 (over x_lo, y, core), tok: 16 (over z, x_hi).
Axes of the slice: x: 4 (x_hi: 2, x_lo: 2; x = x_hi * 2 + x_lo), y: 4, z: 8, core: 2. Of those that a mesh axis runs over, the one named last changes fastest.
Arguments:
- query_acts: bfloat16 [16, 4096, 4096], P('query', 'tok'), may hold values from -6 to 6
- query_grads: bfloat16 [16, 4096, 512], P('query', 'tok'), may hold values from -6 to 6
- sketch_maps: bfloat16 [16, 32, 512], P('query'), may hold values from -0.25 to 0.25
- res_acts: bfloat16 [262144, 4096], P(('query', 'tok')), may hold values from -6 to 6
- res_grads: bfloat16 [262144, 512], P(('query', 'tok')), may hold values from -6 to 6
Outputs:
- scores: float32 [16, 262144], P(None, ('query', 'tok'))
The draws below stay inside these ranges and needn't reach their ends.
All inputs are finite; a program needn't handle non-finite values.
Results may differ from the reference program's by a relative error of at most 0.0054.
Values may be sent and summed in bfloat16 or wider, within the bound.
No kernel may reach another device: no remote copies, remote signals or barrier semaphores. Data moves between devices by JAX's collectives and lax.ppermute only.
A program may use at most 64 MiB of HBM per device.

```python
import math
import jax
import jax.numpy as jnp
from jax import lax

DIN = 4096
DOUT = 512
RANK = 32
RES_DEV = 1024
NQ = 16
QTOK = 4096
RTOK = 262144


def block_levels(own_key, shape, cuts, smallest, high):
    gain, own = 1.0, jax.random.fold_in(own_key, 6)
    for axis_at, blocks in cuts:
        draws = jnp.exp(jax.random.uniform(jax.random.fold_in(own, axis_at), (blocks,), jnp.float32, smallest / len(cuts), high / len(cuts)))
        gain = gain * jnp.repeat(draws, shape[axis_at] // blocks).reshape([-1 if axis == axis_at else 1 for axis in range(len(shape))])
    return gain


def normal_values(stream_key, shape, scale, reach, split=(), kind=jnp.bfloat16):
    gain = block_levels(stream_key, shape, split, -0.22, 0.18) if split else 1.0
    entries = jax.random.normal(stream_key, shape, jnp.float32) * scale * gain
    return jnp.minimum(jnp.maximum(entries, -reach), reach).astype(kind)


def setup_inputs(seed: int = 0) -> dict:
    key_list = jax.random.split(jax.random.key(seed), 6)
    query_acts = normal_values(key_list[0], (NQ, QTOK, DIN), 1.0, 6.0, ((0, 16), (1, 16)))
    query_grads = normal_values(key_list[1], (NQ, QTOK, DOUT), 1.0, 6.0, ((0, 16), (1, 16)))
    sketch_maps = normal_values(key_list[2], (NQ, RANK, DOUT), DOUT ** -0.5, 0.25, ((0, 16),))
    res_acts = normal_values(key_list[3], (RTOK, DIN), 1.0, 6.0, ((0, 256),))
    res_grads = normal_values(key_list[4], (RTOK, DOUT), 1.0, 6.0, ((0, 256),))
    return {"query_acts": query_acts, "query_grads": query_grads, "sketch_maps": sketch_maps, "res_acts": res_acts, "res_grads": res_grads}


def factors(query_act, query_grad, sketch_map):
    projected = lax.dot_general(sketch_map.astype(jnp.float32), query_grad.astype(jnp.float32), (((1,), (1,)), ((), ())), preferred_element_type=jnp.float32).astype(jnp.bfloat16)
    sketch = jnp.dot(projected.astype(jnp.float32), query_act.astype(jnp.float32), preferred_element_type=jnp.float32)
    gram_matrix = jnp.dot(sketch, sketch.T, precision=lax.Precision.HIGHEST)
    lower_factor = jnp.linalg.cholesky(gram_matrix)
    left_factor = lax.linalg.triangular_solve(lower_factor, sketch, left_side=True, lower=True).astype(jnp.bfloat16)
    pulled = lax.dot_general(left_factor.astype(jnp.float32), query_act.astype(jnp.float32), (((1,), (1,)), ((), ())), preferred_element_type=jnp.float32).astype(jnp.bfloat16)
    right_factor = jnp.dot(pulled.astype(jnp.float32), query_grad.astype(jnp.float32), preferred_element_type=jnp.float32).astype(jnp.bfloat16)
    return (left_factor, right_factor)

def reference(query_acts, query_grads, sketch_maps, res_acts, res_grads):
    left_all, right_all = lax.map(lambda items: factors(items[0], items[1], items[2]), (query_acts, query_grads, sketch_maps))
    left_all = left_all.reshape(NQ * RANK, DIN)
    right_all = right_all.reshape(NQ * RANK, DOUT)
    score_scale = 1.0 / math.sqrt(RANK * DOUT * QTOK)
    block_count = RTOK // RES_DEV
    act_blocks = res_acts.reshape(block_count, RES_DEV, DIN)
    grad_blocks = res_grads.reshape(block_count, RES_DEV, DOUT)

    def one_block(items):
        on_left = lax.dot_general(left_all.astype(jnp.float32), items[0].astype(jnp.float32), (((1,), (1,)), ((), ())), preferred_element_type=jnp.float32)
        on_right = lax.dot_general(right_all.astype(jnp.float32), items[1].astype(jnp.float32), (((1,), (1,)), ((), ())), preferred_element_type=jnp.float32)
        product = (on_left * on_right).reshape(NQ, RANK, RES_DEV)
        return lax.optimization_barrier(jnp.sum(product, axis=1)) * score_scale
    blocks = lax.map(one_block, (act_blocks, grad_blocks))
    return jnp.transpose(blocks, (1, 0, 2)).reshape(NQ, RTOK)
```

```python
import math

import jax
import jax.numpy as jnp
from jax import lax
from jax.sharding import Mesh
from jax.sharding import PartitionSpec as P

QUERY = ("xlo", "y", "core")
TOK = ("z", "xhi")
HIGH = lax.Precision.HIGHEST
F32 = jnp.float32
BF16 = jnp.bfloat16


def contract_last(first_arr, second_arr):
    return lax.dot_general(first_arr, second_arr, (((1,), (1,)), ((), ())), preferred_element_type=F32)


def exchange(blocks, axes):
    return lax.all_to_all(blocks, axes, 0, 0, tiled=True)


def spread(block, axes, count):
    return exchange(jnp.broadcast_to(block[None], (count,) + block.shape), axes)


def local(query_acts, query_grads, sketch_maps, res_acts, res_grads):
    acts, grads, sketch_map = query_acts[0], query_grads[0], sketch_maps[0]
    rank, width = sketch_map.shape[0], acts.shape[1]
    groups = lax.axis_size(TOK)
    queries = lax.axis_size(QUERY)
    part = width // groups
    score_scale = 1.0 / math.sqrt(rank * grads.shape[1] * acts.shape[0] * groups)

    projected = contract_last(sketch_map, grads).astype(BF16)
    partial = jnp.dot(projected, acts, preferred_element_type=F32).astype(BF16)
    partial = partial.reshape(rank, groups, part).transpose(1, 0, 2)
    piece = jnp.sum(exchange(partial, TOK).astype(F32), axis=0).astype(BF16)
    sketch = spread(piece, TOK, groups).transpose(1, 0, 2).reshape(rank, width)

    pulled = contract_last(sketch, acts).astype(BF16)
    right_part = jnp.dot(pulled, grads, preferred_element_type=F32).astype(BF16)
    right_parts = spread(right_part, TOK, groups)

    lefts = lax.all_gather(sketch, QUERY, axis=0, tiled=True)
    on_left = contract_last(lefts, res_acts)

    lower = jnp.linalg.cholesky(contract_last(sketch, sketch))
    inverse = lax.linalg.triangular_solve(lower, jnp.eye(rank, dtype=F32), left_side=True, lower=True)
    right = jnp.sum(right_parts.astype(F32), axis=0)
    right = jnp.dot(inverse.T, jnp.dot(inverse, right, precision=HIGH), precision=HIGH)
    rights = spread(right.astype(BF16), QUERY, queries).reshape(queries * rank, -1)
    on_right = contract_last(rights, res_grads)
    product = (on_left * on_right).reshape(queries, rank, -1)
    return jnp.sum(product, axis=1) * score_scale


def solution(mesh):
    fine = Mesh(mesh.devices.reshape(2, 4, 2, 8, 2), QUERY + TOK)
    in_specs = (
        P(QUERY, TOK, None),
        P(QUERY, TOK, None),
        P(QUERY, None, None),
        P(QUERY + TOK, None),
        P(QUERY + TOK, None),
    )
    return jax.shard_map(local, mesh=fine, in_specs=in_specs, out_specs=P(None, QUERY + TOK), check_vma=False)
```

```python
import math

import jax
import jax.numpy as jnp
from jax import lax
from jax.experimental import pallas as pl
from jax.experimental.pallas import tpu as pltpu
from jax.sharding import Mesh
from jax.sharding import PartitionSpec as P

QUERY = ("xlo", "y", "core")
TOK = ("z", "xhi")
HIGH = lax.Precision.HIGHEST
F32 = jnp.float32
BF16 = jnp.bfloat16
VMEM_LIMIT = 28 * 2**20
STREAM_LIMIT = 60 * 2**20
PIECES = 4


def contract_last(first_arr, second_arr):
    return lax.dot_general(first_arr, second_arr, (((1,), (1,)), ((), ())), preferred_element_type=F32)


def params():
    return pltpu.CompilerParams(dimension_semantics=("arbitrary",), vmem_limit_bytes=VMEM_LIMIT)


def cost(flops, num_bytes):
    return pl.CostEstimate(flops=flops, bytes_accessed=num_bytes, transcendentals=0)


def exchange(blocks, axes):
    return lax.all_to_all(blocks, axes, 0, 0, tiled=True)


def swap_cores(block):
    return lax.ppermute(block, "core", [(0, 1), (1, 0)])


def partial_sketch(sketch_maps, query_grads, query_acts, groups):
    projected = contract_last(sketch_maps[0], query_grads[0]).astype(BF16)
    partial = jnp.dot(projected, query_acts[0], preferred_element_type=F32).astype(BF16)
    rank, width = partial.shape
    return partial.reshape(rank, groups, width // groups).transpose(1, 0, 2)


def piece_kernel(parts_ref, out_ref):
    total = jnp.sum(parts_ref[...].astype(F32), axis=0).astype(BF16)
    out_ref[...] = jnp.broadcast_to(total[None], out_ref.shape)


def sum_pieces(parts):
    return pl.pallas_call(
        piece_kernel,
        out_shape=jax.ShapeDtypeStruct(parts.shape, BF16),
        compiler_params=pltpu.CompilerParams(vmem_limit_bytes=VMEM_LIMIT),
    )(parts)


def right_kernel(sketch_ref, acts_ref, grads_ref, out_ref, gram_ref, pulled_ref):
    step = pl.program_id(0)
    blocks, _, part = sketch_ref.shape

    @pl.when(step == 0)
    def _():
        pulled_ref[...] = jnp.zeros_like(pulled_ref)
        gram_ref[...] = jnp.zeros_like(gram_ref)

    for i in range(blocks):
        block = sketch_ref[i]
        pulled_ref[...] += contract_last(acts_ref[0, :, i * part : (i + 1) * part], block)
        gram_ref[...] += contract_last(block, block)

    @pl.when(step == pl.num_programs(0) - 1)
    def _():
        pulled = pulled_ref[...].T.astype(BF16)
        right = jnp.dot(pulled, grads_ref[0], preferred_element_type=F32)
        out_ref[...] = jnp.broadcast_to(right.astype(BF16)[None], out_ref.shape)


def partial_right(sketch, query_acts, query_grads):
    groups, rank, part = sketch.shape
    _, tokens, width = query_acts.shape
    outs = query_grads.shape[2]
    steps = 4
    return pl.pallas_call(
        right_kernel,
        grid=(steps,),
        in_specs=[
            pl.BlockSpec((groups // steps, rank, part), lambda i: (i, 0, 0)),
            pl.BlockSpec((1, tokens, width // steps), lambda i: (0, 0, i)),
            pl.BlockSpec((1, tokens, outs), lambda i: (0, 0, 0)),
        ],
        out_specs=[
            pl.BlockSpec((groups, rank, outs), lambda i: (0, 0, 0)),
            pl.BlockSpec((rank, rank), lambda i: (0, 0)),
        ],
        out_shape=[
            jax.ShapeDtypeStruct((groups, rank, outs), BF16),
            jax.ShapeDtypeStruct((rank, rank), F32),
        ],
        scratch_shapes=[pltpu.VMEM((tokens, rank), F32)],
        compiler_params=params(),
        cost_estimate=cost(2 * rank * tokens * (width + outs), 2 * tokens * (width + outs)),
    )(sketch, query_acts, query_grads)


def solve_kernel(parts_ref, inverse_ref, out_ref):
    total = jnp.sum(parts_ref[...].astype(F32), axis=0)
    inverse = inverse_ref[...]
    half = jnp.dot(inverse, total, precision=HIGH, preferred_element_type=F32)
    full = lax.dot_general(inverse, half, (((0,), (0,)), ((), ())), precision=HIGH, preferred_element_type=F32)
    out_ref[...] = jnp.broadcast_to(full.astype(BF16)[None], out_ref.shape)


def solve_right(parts, inverse, queries):
    _, rank, outs = parts.shape
    return pl.pallas_call(
        solve_kernel,
        out_shape=jax.ShapeDtypeStruct((queries, rank, outs), BF16),
        compiler_params=pltpu.CompilerParams(vmem_limit_bytes=VMEM_LIMIT),
    )(parts, inverse)


def stack_rows(near_ref, far_ref):
    chips, blocks, rank, part = near_ref.shape

    def rows(i):
        return jnp.concatenate([ref[:, i].reshape(chips * rank, part) for ref in (near_ref, far_ref)], axis=0)

    return jnp.concatenate([rows(i) for i in range(blocks)], axis=1)


def row_copies(acts_ref, held_ref, sems):
    pieces, height, _ = held_ref.shape
    return [
        pltpu.make_async_copy(acts_ref.at[pl.ds(i * height, height)], held_ref.at[i], sems.at[i])
        for i in range(pieces)
    ]


def row_scratch(res_acts):
    tokens, width = res_acts.shape
    return [pltpu.VMEM((PIECES, tokens // PIECES, width), BF16), pltpu.SemaphoreType.DMA((PIECES,))]


def whole_copies(refs, held_refs, sems):
    return [pltpu.make_async_copy(ref, held, sems.at[i]) for i, (ref, held) in enumerate(zip(refs, held_refs))]


def whole_scratch(*arrays):
    return [pltpu.VMEM(x.shape, x.dtype) for x in arrays] + [pltpu.SemaphoreType.DMA((len(arrays),))]


def left_kernel(near_ref, far_ref, acts_ref, out_ref, held_ref, sems, near_held_ref, far_held_ref, pair_sems):
    pair = whole_copies((near_ref, far_ref), (near_held_ref, far_held_ref), pair_sems)
    copies = row_copies(acts_ref, held_ref, sems)
    for copy in pair + copies:
        copy.start()
    for copy in pair:
        copy.wait()
    rows = stack_rows(near_held_ref, far_held_ref)
    height = held_ref.shape[1]
    for i, copy in enumerate(copies):
        copy.wait()
        out_ref[i * height : (i + 1) * height] = contract_last(held_ref[i], rows)


def on_left(near, far, res_acts):
    rows, tokens = 2 * near.shape[0] * near.shape[2], res_acts.shape[0]
    return pl.pallas_call(
        left_kernel,
        in_specs=[pl.BlockSpec(memory_space=pl.ANY)] * 3,
        out_specs=pl.BlockSpec(memory_space=pltpu.VMEM),
        out_shape=jax.ShapeDtypeStruct((tokens, rows), F32),
        scratch_shapes=row_scratch(res_acts) + whole_scratch(near, far),
        compiler_params=pltpu.CompilerParams(vmem_limit_bytes=STREAM_LIMIT),
        cost_estimate=cost(0, 0),
    )(near, far, res_acts)


def sum_ranks(product, queries, rank):
    shape = (queries, queries * rank)
    owner = lax.broadcasted_iota(jnp.int32, shape, 1) // rank
    chosen = (owner == lax.broadcasted_iota(jnp.int32, shape, 0)).astype(BF16)
    total = 0.0
    for _ in range(3):
        term = product.astype(BF16)
        total = total + contract_last(chosen, term)
        product = product - term.astype(F32)
    return total


def make_score_kernel(score_scale):
    def score_kernel(order_ref, *refs):
        (near_ref, far_ref, own_ref, rights_ref, grads_ref, acts_ref, out_ref), refs = refs[:7], refs[7:]
        (held_ref, sems, sorted_ref, near_held_ref, far_held_ref, own_held_ref, rights_held_ref, grads_held_ref), refs = (
            refs[:8],
            refs[8:],
        )
        near_copy, far_copy, own_copy, rights_copy, grads_copy = whole_copies(
            (near_ref, far_ref, own_ref, rights_ref, grads_ref),
            (near_held_ref, far_held_ref, own_held_ref, rights_held_ref, grads_held_ref),
            refs[0],
        )
        copies = row_copies(acts_ref, held_ref, sems)
        for copy in [rights_copy, grads_copy, near_copy, far_copy] + copies + [own_copy]:
            copy.start()

        queries, rank, outs = rights_ref.shape
        half = queries // 2
        height = held_ref.shape[1]
        rights_copy.wait()
        for i in range(queries):
            sorted_ref[i] = rights_held_ref[order_ref[i]]
        grads_copy.wait()
        on_right = contract_last(grads_held_ref[...], sorted_ref[...].reshape(queries * rank, outs))

        near_copy.wait()
        far_copy.wait()
        rows = stack_rows(near_held_ref, far_held_ref)
        for j, copy in enumerate(copies):
            copy.wait()
            tokens = slice(j * height, (j + 1) * height)
            product = contract_last(held_ref[j], rows) * on_right[tokens, half * rank :]
            other = sum_ranks(product, half, rank) * score_scale
            for i in range(half):
                out_ref[pl.ds(order_ref[half + i], 1), tokens] = other[i : i + 1]

        own_copy.wait()
        own = sum_ranks(own_held_ref[...] * on_right[:, : half * rank], half, rank) * score_scale
        for i in range(half):
            out_ref[pl.ds(order_ref[i], 1), :] = own[i : i + 1]

    return score_kernel


def all_scores(order, near, far, res_acts, own, rights, res_grads, score_scale):
    tokens, rows = own.shape
    queries = rights.shape[0]
    return pl.pallas_call(
        make_score_kernel(score_scale),
        in_specs=[pl.BlockSpec(memory_space=pltpu.SMEM)] + [pl.BlockSpec(memory_space=pl.ANY)] * 6,
        out_specs=pl.BlockSpec(memory_space=pltpu.VMEM),
        out_shape=jax.ShapeDtypeStruct((queries, tokens), F32),
        scratch_shapes=row_scratch(res_acts)
        + [pltpu.VMEM(rights.shape, BF16)]
        + whole_scratch(near, far, own, rights, res_grads),
        compiler_params=pltpu.CompilerParams(vmem_limit_bytes=STREAM_LIMIT),
        cost_estimate=cost(2 * rows * (res_acts.size + 2 * res_grads.size), 2 * res_acts.size),
    )(order, near, far, own, rights, res_grads, res_acts)


def from_back(block, axis, step):
    size = lax.axis_size(axis)
    return lax.ppermute(block, axis, [(i, (i + step) % size) for i in range(size)])


NEAR = ((0, 0), (1, 0), (0, 1), (0, 3))
FAR = ((1, 1), (1, 3), (0, 2), (1, 2))


def local(query_acts, query_grads, sketch_maps, res_acts, res_grads):
    rank, outs = sketch_maps.shape[1:]
    groups, queries = lax.axis_size(TOK), lax.axis_size(QUERY)
    score_scale = 1.0 / math.sqrt(rank * outs * query_acts.shape[1] * groups)

    parts = exchange(partial_sketch(sketch_maps, query_grads, query_acts, groups), TOK)
    sketch = exchange(sum_pieces(parts), TOK)
    right_part, gram = partial_right(sketch, query_acts, query_grads)
    sketch, right_part = lax.optimization_barrier((sketch, right_part))
    right_parts = exchange(right_part, TOK)

    lower = jnp.linalg.cholesky(gram)
    inverse = lax.linalg.triangular_solve(lower, jnp.eye(rank, dtype=F32), left_side=True, lower=True)
    right = solve_right(right_parts, inverse, queries)

    rights = exchange(right, QUERY)

    beside = from_back(sketch, "xlo", 1)
    behind, ahead = from_back(sketch, "y", 1), from_back(sketch, "y", 3)
    near = jnp.stack([sketch, beside, behind, ahead])
    other_near = swap_cores(near)
    corners = [from_back(beside, "y", 1), from_back(beside, "y", 3)]
    across = [from_back(behind, "y", 1), from_back(corners[1], "y", 3)]
    _, corners, across = lax.optimization_barrier((right, corners, across))
    far = jnp.stack(corners + across)
    other_far = swap_cores(far)

    wide, high = lax.axis_size("xlo"), lax.axis_size("y")
    column, row = lax.axis_index("xlo"), lax.axis_index("y")
    place = [(column + wide - x) % wide * high + (row + high - y) % high for x, y in NEAR + FAR]
    place = 2 * jnp.stack(place).astype(jnp.int32)
    core = lax.axis_index("core").astype(jnp.int32)
    order = jnp.concatenate([place + core, place + 1 - core])

    own_left = on_left(near, far, res_acts)
    return all_scores(order, other_near, other_far, res_acts, own_left, rights, res_grads, score_scale)


def solution(mesh):
    fine = Mesh(mesh.devices.reshape(2, 4, 2, 8, 2), QUERY + TOK)
    in_specs = (
        P(QUERY, TOK, None),
        P(QUERY, TOK, None),
        P(QUERY, None, None),
        P(QUERY + TOK, None),
        P(QUERY + TOK, None),
    )
    return jax.shard_map(local, mesh=fine, in_specs=in_specs, out_specs=P(None, QUERY + TOK), check_vma=False)
```

```python
import math

import jax
import jax.numpy as jnp
from jax import lax
from jax.experimental import pallas as pl
from jax.experimental.pallas import tpu as pltpu
from jax.sharding import Mesh
from jax.sharding import PartitionSpec as P

QUERY = ("xlo", "y", "core")
TOK = ("z", "xhi")
HIGH = lax.Precision.HIGHEST
F32 = jnp.float32
BF16 = jnp.bfloat16
VMEM_LIMIT = 12 * 2**20


def contract_last(first_arr, second_arr):
    return lax.dot_general(first_arr, second_arr, (((1,), (1,)), ((), ())), preferred_element_type=F32)


def cost(flops, num_bytes):
    return pl.CostEstimate(flops=flops, bytes_accessed=num_bytes, transcendentals=0)


def exchange(blocks, axes):
    return lax.all_to_all(blocks, axes, 0, 0, tiled=True)


def swap_cores(block):
    return lax.ppermute(block, "core", [(0, 1), (1, 0)])


def stack_rows(refs):
    blocks = range(refs[0].shape[0])
    return jnp.concatenate([jnp.concatenate([ref[i] for ref in refs], axis=0) for i in blocks], axis=1)


def partial_sketch(sketch_maps, query_grads, query_acts, groups):
    projected = contract_last(sketch_maps[0], query_grads[0]).astype(BF16)
    partial = jnp.dot(projected, query_acts[0], preferred_element_type=F32).astype(BF16)
    rank, width = partial.shape
    return partial.reshape(rank, groups, width // groups).transpose(1, 0, 2)


def piece_kernel(parts_ref, out_ref):
    total = jnp.sum(parts_ref[...].astype(F32), axis=0).astype(BF16)
    out_ref[...] = jnp.broadcast_to(total[None], out_ref.shape)


def sum_pieces(parts):
    return pl.pallas_call(
        piece_kernel,
        out_shape=jax.ShapeDtypeStruct(parts.shape, BF16),
        compiler_params=pltpu.CompilerParams(vmem_limit_bytes=VMEM_LIMIT),
    )(parts)


def right_kernel(sketch_ref, acts_ref, grads_ref, out_ref, gram_ref):
    sketch = stack_rows([sketch_ref])
    pulled = contract_last(acts_ref[0], sketch)
    gram_ref[...] = contract_last(sketch, sketch)
    right = jnp.dot(pulled.T.astype(BF16), grads_ref[0], preferred_element_type=F32)
    out_ref[...] = jnp.broadcast_to(right.astype(BF16)[None], out_ref.shape)


def partial_right(sketch, query_acts, query_grads):
    groups, rank, _ = sketch.shape
    outs = query_grads.shape[2]
    vmem = pl.BlockSpec(memory_space=pltpu.VMEM)
    return pl.pallas_call(
        right_kernel,
        in_specs=[vmem] * 3,
        out_specs=[vmem] * 2,
        out_shape=[
            jax.ShapeDtypeStruct((groups, rank, outs), BF16),
            jax.ShapeDtypeStruct((rank, rank), F32),
        ],
        compiler_params=pltpu.CompilerParams(vmem_limit_bytes=VMEM_LIMIT),
        cost_estimate=cost(2 * rank * (query_acts.size + query_grads.size), 2 * query_acts.size),
    )(sketch, query_acts, query_grads)


def inverse_kernel(gram_ref, out_ref):
    rank = gram_ref.shape[0]
    row = lax.broadcasted_iota(jnp.int32, (rank, 2 * rank), 0)
    column = lax.broadcasted_iota(jnp.int32, (rank, 2 * rank), 1)
    unit = (column - rank == row).astype(F32)
    pair = jnp.concatenate([gram_ref[...], unit[:, rank:]], axis=1)
    for i in range(rank):
        pivot = pair[i : i + 1] / pair[i : i + 1, i : i + 1]
        pair = jnp.where(row == i, pivot, pair - pair[:, i : i + 1] * pivot)
    out_ref[...] = pair[:, rank:]


def invert(gram):
    return pl.pallas_call(
        inverse_kernel,
        out_shape=jax.ShapeDtypeStruct(gram.shape, F32),
        compiler_params=pltpu.CompilerParams(vmem_limit_bytes=VMEM_LIMIT),
        cost_estimate=cost(2**32, 2**22),
    )(gram)


def solve_kernel(parts_ref, inverse_ref, out_ref):
    total = jnp.sum(parts_ref[...].astype(F32), axis=0)
    out_ref[...] = jnp.dot(inverse_ref[...], total, precision=HIGH, preferred_element_type=F32).astype(BF16)


def solve_right(parts, inverse):
    return pl.pallas_call(
        solve_kernel,
        out_shape=jax.ShapeDtypeStruct(parts.shape[1:], BF16),
        compiler_params=pltpu.CompilerParams(vmem_limit_bytes=VMEM_LIMIT),
        cost_estimate=cost(0, 0),
    )(parts, inverse)


def touch_kernel(acts_ref, out_ref):
    out_ref[...] = acts_ref[: out_ref.shape[0], : out_ref.shape[1]]


def touch(res_acts):
    vmem = pl.BlockSpec(memory_space=pltpu.VMEM)
    return pl.pallas_call(
        touch_kernel,
        in_specs=[vmem],
        out_specs=vmem,
        out_shape=jax.ShapeDtypeStruct((16, 128), res_acts.dtype),
        compiler_params=pltpu.CompilerParams(vmem_limit_bytes=VMEM_LIMIT),
        cost_estimate=cost(0, 2 * res_acts.size),
    )(res_acts)


def left_kernel(acts_ref, token_ref, *refs):
    refs[-1][...] = contract_last(acts_ref[...], stack_rows(refs[:-1]))


def on_left(sketches, res_acts, token):
    rows, tokens = len(sketches) * sketches[0].shape[1], res_acts.shape[0]
    return pl.pallas_call(
        left_kernel,
        in_specs=[pl.BlockSpec(memory_space=pltpu.VMEM)] * (2 + len(sketches)),
        out_specs=pl.BlockSpec(memory_space=pltpu.VMEM),
        out_shape=jax.ShapeDtypeStruct((tokens, rows), F32),
        compiler_params=pltpu.CompilerParams(vmem_limit_bytes=VMEM_LIMIT),
        cost_estimate=cost(0, 0),
    )(res_acts, token, *sketches)


def sum_ranks(product, first, queries, rank):
    shape = (product.shape[1], queries)
    chosen = lax.broadcasted_iota(jnp.int32, shape, 0) // rank + first == lax.broadcasted_iota(jnp.int32, shape, 1)
    chosen = chosen.astype(F32).astype(BF16)
    total = 0.0
    for _ in range(3):
        term = product.astype(BF16)
        total = total + jnp.dot(term, chosen, preferred_element_type=F32)
        product = product - term.astype(F32)
    return total


def make_score_kernel(score_scale, wide, high):
    def score_kernel(place_ref, own_ref, other_ref, grads_ref, *refs):
        rights, out_ref = refs[:-1], refs[-1]
        queries = out_ref.shape[0]
        half, rank = queries // 2, rights[0].shape[1]
        place = place_ref[0]
        core, row, column = place % 2, place // 2 % high, place // (2 * high)
        chips = [(column + wide - x) % wide * high + (row + high - y) % high for x, y in STEPS]
        order = [2 * chip + core for chip in chips] + [2 * chip + 1 - core for chip in chips]
        total = 0.0
        for j, left_ref in enumerate((own_ref, other_ref)):
            right = jnp.concatenate([ref[i] for ref in rights for i in range(j, ref.shape[0], 2)], axis=0)
            product = left_ref[...] * contract_last(grads_ref[...], right)
            total = total + sum_ranks(product, j * half, queries, rank)
        sums = total.T * score_scale
        for i, query in enumerate(order):
            out_ref[pl.ds(query, 1), :] = sums[i : i + 1]

    return score_kernel


def all_scores(place, own, other, rights, res_grads, score_scale, sizes):
    queries = sum(x.shape[0] for x in rights)
    vmem = pl.BlockSpec(memory_space=pltpu.VMEM)
    return pl.pallas_call(
        make_score_kernel(score_scale, *sizes),
        in_specs=[pl.BlockSpec(memory_space=pltpu.SMEM)] + [vmem] * (3 + len(rights)),
        out_specs=vmem,
        out_shape=jax.ShapeDtypeStruct((queries, own.shape[0]), F32),
        compiler_params=pltpu.CompilerParams(vmem_limit_bytes=VMEM_LIMIT),
        cost_estimate=cost(2 * own.size * res_grads.shape[1], 2 * res_grads.size),
    )(place, own, other, res_grads, *rights)


def from_back(block, axis, step):
    size = lax.axis_size(axis)
    return lax.ppermute(block, axis, [(i, (i + step) % size) for i in range(size)])


STEPS = ((0, 0), (1, 0), (0, 1), (1, 1), (0, 3), (1, 3), (0, 2), (1, 2))


def local(query_acts, query_grads, sketch_maps, res_acts, res_grads):
    rank, outs = sketch_maps.shape[1:]
    groups = lax.axis_size(TOK)
    score_scale = 1.0 / math.sqrt(rank * outs * query_acts.shape[1] * groups)

    parts = exchange(partial_sketch(sketch_maps, query_grads, query_acts, groups), TOK)
    sketch = exchange(sum_pieces(parts), TOK)
    place = lax.axis_index(QUERY).astype(jnp.int32).reshape(1)
    sketch, place = lax.optimization_barrier((sketch, place))
    right_part, gram = partial_right(sketch, query_acts, query_grads)
    sketch, right_part = lax.optimization_barrier((sketch, right_part))
    right_parts = exchange(right_part, TOK)

    inverse = invert(gram)
    right = solve_right(right_parts, inverse)

    beside, behind, ahead = from_back(sketch, "xlo", 1), from_back(sketch, "y", 1), from_back(sketch, "y", 3)
    _, beside, behind = lax.optimization_barrier((inverse, beside, behind))
    corners = [from_back(beside, "y", 1), from_back(beside, "y", 3)]
    across = [from_back(behind, "y", 1), from_back(corners[1], "y", 3)]
    right, ahead = lax.optimization_barrier((right, ahead))
    both = jnp.stack([right, swap_cores(right)])
    early = [sketch, beside, behind, corners[0], ahead, corners[1], across[0]]
    both, acts, *early = lax.optimization_barrier((both, res_acts, *early))
    both = jnp.concatenate([both, from_back(both, "xlo", 1)])
    other_early = [swap_cores(block) for block in early[:4]]
    both, token, *later = lax.optimization_barrier((both, touch(acts), *early[4:]))
    other_early += [swap_cores(block) for block in later]
    rights = [both] + [from_back(both, "y", step) for step in (1, 3, 2)]
    token, last, *early = lax.optimization_barrier((token, across[1], *early))
    own_left = on_left(early + [last], acts, token)
    other_left = on_left(other_early + [swap_cores(last)], acts, token)
    sizes = lax.axis_size("xlo"), lax.axis_size("y")
    return all_scores(place, own_left, other_left, rights, res_grads, score_scale, sizes)


def solution(mesh):
    fine = Mesh(mesh.devices.reshape(2, 4, 2, 8, 2), QUERY + TOK)
    in_specs = (
        P(QUERY, TOK, None),
        P(QUERY, TOK, None),
        P(QUERY, None, None),
        P(QUERY + TOK, None),
        P(QUERY + TOK, None),
    )
    return jax.shard_map(local, mesh=fine, in_specs=in_specs, out_specs=P(None, QUERY + TOK), check_vma=False)
```

```python
import math

import jax
import jax.numpy as jnp
from jax import lax
from jax.experimental import pallas as pl
from jax.experimental.pallas import tpu as pltpu
from jax.sharding import Mesh
from jax.sharding import PartitionSpec as P

QUERY = ("xlo", "y", "core")
TOK = ("z", "xhi")
HIGH = lax.Precision.HIGHEST
F32 = jnp.float32
BF16 = jnp.bfloat16
VMEM_LIMIT = 12 * 2**20


def contract_last(first_arr, second_arr):
    return lax.dot_general(first_arr, second_arr, (((1,), (1,)), ((), ())), preferred_element_type=F32)


def cost(flops, num_bytes):
    return pl.CostEstimate(flops=flops, bytes_accessed=num_bytes, transcendentals=0)


def exchange(blocks, axes):
    return lax.all_to_all(blocks, axes, 0, 0, tiled=True)


def swap_cores(block):
    return lax.ppermute(block, "core", [(0, 1), (1, 0)])


def stack_rows(refs):
    blocks = range(refs[0].shape[0])
    return jnp.concatenate([jnp.concatenate([ref[i] for ref in refs], axis=0) for i in blocks], axis=1)


def partial_sketch(sketch_maps, query_grads, query_acts, groups):
    projected = contract_last(sketch_maps[0], query_grads[0]).astype(BF16)
    partial = jnp.dot(projected, query_acts[0], preferred_element_type=F32).astype(BF16)
    rank, width = partial.shape
    return partial.reshape(rank, groups, width // groups).transpose(1, 0, 2)


def piece_kernel(parts_ref, out_ref):
    total = jnp.sum(parts_ref[...].astype(F32), axis=0).astype(BF16)
    out_ref[...] = jnp.broadcast_to(total[None], out_ref.shape)


def sum_pieces(parts):
    return pl.pallas_call(
        piece_kernel,
        out_shape=jax.ShapeDtypeStruct(parts.shape, BF16),
        compiler_params=pltpu.CompilerParams(vmem_limit_bytes=VMEM_LIMIT),
    )(parts)


def right_kernel(sketch_ref, acts_ref, grads_ref, out_ref, gram_ref):
    sketch = stack_rows([sketch_ref])
    pulled = contract_last(acts_ref[0], sketch)
    gram_ref[...] = contract_last(sketch, sketch)
    right = jnp.dot(pulled.T.astype(BF16), grads_ref[0], preferred_element_type=F32)
    out_ref[...] = jnp.broadcast_to(right.astype(BF16)[None], out_ref.shape)


def partial_right(sketch, query_acts, query_grads):
    groups, rank, _ = sketch.shape
    outs = query_grads.shape[2]
    vmem = pl.BlockSpec(memory_space=pltpu.VMEM)
    return pl.pallas_call(
        right_kernel,
        in_specs=[vmem] * 3,
        out_specs=[vmem] * 2,
        out_shape=[
            jax.ShapeDtypeStruct((groups, rank, outs), BF16),
            jax.ShapeDtypeStruct((rank, rank), F32),
        ],
        compiler_params=pltpu.CompilerParams(vmem_limit_bytes=VMEM_LIMIT),
        cost_estimate=cost(2 * rank * (query_acts.size + query_grads.size), 2 * query_acts.size),
    )(sketch, query_acts, query_grads)


def inverse_kernel(gram_ref, out_ref):
    rank = gram_ref.shape[0]
    row = lax.broadcasted_iota(jnp.int32, (rank, 2 * rank), 0)
    column = lax.broadcasted_iota(jnp.int32, (rank, 2 * rank), 1)
    unit = (column - rank == row).astype(F32)
    pair = jnp.concatenate([gram_ref[...], unit[:, rank:]], axis=1)
    for i in range(rank):
        pivot = pair[i : i + 1] / pair[i : i + 1, i : i + 1]
        pair = jnp.where(row == i, pivot, pair - pair[:, i : i + 1] * pivot)
    out_ref[...] = pair[:, rank:]


def invert(gram):
    return pl.pallas_call(
        inverse_kernel,
        out_shape=jax.ShapeDtypeStruct(gram.shape, F32),
        compiler_params=pltpu.CompilerParams(vmem_limit_bytes=VMEM_LIMIT),
        cost_estimate=cost(2**32, 2**22),
    )(gram)


def solve_kernel(parts_ref, inverse_ref, out_ref):
    total = jnp.sum(parts_ref[...].astype(F32), axis=0)
    out_ref[...] = jnp.dot(inverse_ref[...], total, precision=HIGH, preferred_element_type=F32).astype(BF16)


def solve_right(parts, inverse):
    return pl.pallas_call(
        solve_kernel,
        out_shape=jax.ShapeDtypeStruct(parts.shape[1:], BF16),
        compiler_params=pltpu.CompilerParams(vmem_limit_bytes=VMEM_LIMIT),
        cost_estimate=cost(0, 0),
    )(parts, inverse)


def touch_kernel(acts_ref, out_ref):
    out_ref[...] = acts_ref[: out_ref.shape[0], : out_ref.shape[1]]


def touch(res_acts):
    vmem = pl.BlockSpec(memory_space=pltpu.VMEM)
    return pl.pallas_call(
        touch_kernel,
        in_specs=[vmem],
        out_specs=vmem,
        out_shape=jax.ShapeDtypeStruct((16, 128), res_acts.dtype),
        compiler_params=pltpu.CompilerParams(vmem_limit_bytes=VMEM_LIMIT),
        cost_estimate=cost(0, 2 * res_acts.size),
    )(res_acts)


def left_kernel(acts_ref, token_ref, *refs):
    refs[-1][...] = contract_last(acts_ref[...], stack_rows(refs[:-1]))


def on_left(sketches, res_acts, token):
    rows, tokens = len(sketches) * sketches[0].shape[1], res_acts.shape[0]
    return pl.pallas_call(
        left_kernel,
        in_specs=[pl.BlockSpec(memory_space=pltpu.VMEM)] * (2 + len(sketches)),
        out_specs=pl.BlockSpec(memory_space=pltpu.VMEM),
        out_shape=jax.ShapeDtypeStruct((tokens, rows), F32),
        compiler_params=pltpu.CompilerParams(vmem_limit_bytes=VMEM_LIMIT),
        cost_estimate=cost(0, 0),
    )(res_acts, token, *sketches)


def sum_ranks(product, first, queries, rank):
    shape = (product.shape[1], queries)
    chosen = lax.broadcasted_iota(jnp.int32, shape, 0) // rank + first == lax.broadcasted_iota(jnp.int32, shape, 1)
    chosen = chosen.astype(F32).astype(BF16)
    total = 0.0
    for _ in range(2):
        term = product.astype(BF16)
        total = total + jnp.dot(term, chosen, preferred_element_type=F32)
        product = product - term.astype(F32)
    return total


def make_score_kernel(score_scale, wide, high):
    def score_kernel(place_ref, own_ref, other_ref, grads_ref, *refs):
        rights, out_ref = refs[:-1], refs[-1]
        queries = out_ref.shape[0]
        half, rank = queries // 2, rights[0].shape[1]
        place = place_ref[0]
        core, row, column = place % 2, place // 2 % high, place // (2 * high)
        chips = [(column + wide - x) % wide * high + (row + high - y) % high for x, y in STEPS]
        order = [2 * chip + core for chip in chips] + [2 * chip + 1 - core for chip in chips]
        total = 0.0
        for j, left_ref in enumerate((own_ref, other_ref)):
            right = jnp.concatenate([ref[i] for ref in rights for i in range(j, ref.shape[0], 2)], axis=0)
            product = left_ref[...] * contract_last(grads_ref[...], right)
            total = total + sum_ranks(product, j * half, queries, rank)
        sums = total.T * score_scale
        for i, query in enumerate(order):
            out_ref[pl.ds(query, 1), :] = sums[i : i + 1]

    return score_kernel


def all_scores(place, own, other, rights, res_grads, score_scale, sizes):
    queries = sum(x.shape[0] for x in rights)
    vmem = pl.BlockSpec(memory_space=pltpu.VMEM)
    return pl.pallas_call(
        make_score_kernel(score_scale, *sizes),
        in_specs=[pl.BlockSpec(memory_space=pltpu.SMEM)] + [vmem] * (3 + len(rights)),
        out_specs=vmem,
        out_shape=jax.ShapeDtypeStruct((queries, own.shape[0]), F32),
        compiler_params=pltpu.CompilerParams(vmem_limit_bytes=VMEM_LIMIT),
        cost_estimate=cost(2 * own.size * res_grads.shape[1], 2 * res_grads.size),
    )(place, own, other, res_grads, *rights)


def from_back(block, axis, step):
    size = lax.axis_size(axis)
    return lax.ppermute(block, axis, [(i, (i + step) % size) for i in range(size)])


STEPS = ((0, 0), (1, 0), (0, 1), (1, 1), (0, 3), (1, 3), (0, 2), (1, 2))


def local(query_acts, query_grads, sketch_maps, res_acts, res_grads):
    rank, outs = sketch_maps.shape[1:]
    groups = lax.axis_size(TOK)
    score_scale = 1.0 / math.sqrt(rank * outs * query_acts.shape[1] * groups)

    place = lax.axis_index(QUERY).astype(jnp.int32).reshape(1)
    partial = partial_sketch(sketch_maps, query_grads, query_acts, groups)
    partial, place = lax.optimization_barrier((partial, place))
    parts = exchange(partial, TOK)
    sketch = exchange(sum_pieces(parts), TOK)
    right_part, gram = partial_right(sketch, query_acts, query_grads)
    sketch, right_part = lax.optimization_barrier((sketch, right_part))
    right_parts = exchange(right_part, TOK)

    inverse = invert(gram)
    right = solve_right(right_parts, inverse)

    beside, behind, ahead = from_back(sketch, "xlo", 1), from_back(sketch, "y", 1), from_back(sketch, "y", 3)
    _, beside, behind = lax.optimization_barrier((inverse, beside, behind))
    corners = [from_back(beside, "y", 1), from_back(beside, "y", 3)]
    across = [from_back(behind, "y", 1), from_back(corners[1], "y", 3)]
    right, ahead = lax.optimization_barrier((right, ahead))
    both = jnp.stack([right, swap_cores(right)])
    early = [sketch, beside, behind, corners[0], ahead, corners[1], across[0]]
    both, acts, *early = lax.optimization_barrier((both, res_acts, *early))
    both = jnp.concatenate([both, from_back(both, "xlo", 1)])
    other_early = [swap_cores(block) for block in early[:4]]
    both, token, *later = lax.optimization_barrier((both, touch(acts), *early[4:]))
    other_early += [swap_cores(block) for block in later]
    rights = [both] + [from_back(both, "y", step) for step in (1, 3, 2)]
    token, last, *early = lax.optimization_barrier((token, across[1], *early))
    own_left = on_left(early + [last], acts, token)
    other_left = on_left(other_early + [swap_cores(last)], acts, token)
    sizes = lax.axis_size("xlo"), lax.axis_size("y")
    return all_scores(place, own_left, other_left, rights, res_grads, score_scale, sizes)


def solution(mesh):
    fine = Mesh(mesh.devices.reshape(2, 4, 2, 8, 2), QUERY + TOK)
    in_specs = (
        P(QUERY, TOK, None),
        P(QUERY, TOK, None),
        P(QUERY, None, None),
        P(QUERY + TOK, None),
        P(QUERY + TOK, None),
    )
    return jax.shard_map(local, mesh=fine, in_specs=in_specs, out_specs=P(None, QUERY + TOK), check_vma=False)
```

```python
import math

import jax
import jax.numpy as jnp
from jax import lax
from jax.experimental import pallas as pl
from jax.experimental.pallas import tpu as pltpu
from jax.sharding import Mesh
from jax.sharding import PartitionSpec as P

QUERY = ("xlo", "y", "core")
TOK = ("z", "xhi")
HIGH = lax.Precision.HIGHEST
F32 = jnp.float32
BF16 = jnp.bfloat16
VMEM_LIMIT = 12 * 2**20


def contract_last(first_arr, second_arr):
    return lax.dot_general(first_arr, second_arr, (((1,), (1,)), ((), ())), preferred_element_type=F32)


def cost(flops, num_bytes):
    return pl.CostEstimate(flops=flops, bytes_accessed=num_bytes, transcendentals=0)


def exchange(blocks, axes):
    return lax.all_to_all(blocks, axes, 0, 0, tiled=True)


def swap_cores(block):
    return lax.ppermute(block, "core", [(0, 1), (1, 0)])


def stack_rows(refs):
    blocks = range(refs[0].shape[0])
    return jnp.concatenate([jnp.concatenate([ref[i] for ref in refs], axis=0) for i in blocks], axis=1)


def partial_sketch(sketch_maps, query_grads, query_acts, groups):
    projected = contract_last(sketch_maps[0], query_grads[0]).astype(BF16)
    partial = jnp.dot(projected, query_acts[0], preferred_element_type=F32).astype(BF16)
    rank, width = partial.shape
    return partial.reshape(rank, groups, width // groups).transpose(1, 0, 2)


def piece_kernel(parts_ref, out_ref):
    total = jnp.sum(parts_ref[...].astype(F32), axis=0).astype(BF16)
    out_ref[...] = jnp.broadcast_to(total[None], out_ref.shape)


def sum_pieces(parts):
    return pl.pallas_call(
        piece_kernel,
        out_shape=jax.ShapeDtypeStruct(parts.shape, BF16),
        compiler_params=pltpu.CompilerParams(vmem_limit_bytes=VMEM_LIMIT),
    )(parts)


def right_kernel(sketch_ref, acts_ref, grads_ref, out_ref, gram_ref):
    sketch = stack_rows([sketch_ref])
    pulled = contract_last(acts_ref[0], sketch)
    gram_ref[...] = contract_last(sketch, sketch)
    right = jnp.dot(pulled.T.astype(BF16), grads_ref[0], preferred_element_type=F32)
    out_ref[...] = jnp.broadcast_to(right.astype(BF16)[None], out_ref.shape)


def partial_right(sketch, query_acts, query_grads):
    groups, rank, _ = sketch.shape
    outs = query_grads.shape[2]
    vmem = pl.BlockSpec(memory_space=pltpu.VMEM)
    return pl.pallas_call(
        right_kernel,
        in_specs=[vmem] * 3,
        out_specs=[vmem] * 2,
        out_shape=[
            jax.ShapeDtypeStruct((groups, rank, outs), BF16),
            jax.ShapeDtypeStruct((rank, rank), F32),
        ],
        compiler_params=pltpu.CompilerParams(vmem_limit_bytes=VMEM_LIMIT),
        cost_estimate=cost(2 * rank * (query_acts.size + query_grads.size), 2 * query_acts.size),
    )(sketch, query_acts, query_grads)


def inverse_kernel(gram_ref, out_ref):
    rank = gram_ref.shape[0]
    row = lax.broadcasted_iota(jnp.int32, (rank, 2 * rank), 0)
    column = lax.broadcasted_iota(jnp.int32, (rank, 2 * rank), 1)
    unit = (column - rank == row).astype(F32)
    pair = jnp.concatenate([gram_ref[...], unit[:, rank:]], axis=1)
    for i in range(rank):
        pivot = pair[i : i + 1] / pair[i : i + 1, i : i + 1]
        pair = jnp.where(row == i, pivot, pair - pair[:, i : i + 1] * pivot)
    out_ref[...] = pair[:, rank:]


def invert(gram):
    return pl.pallas_call(
        inverse_kernel,
        out_shape=jax.ShapeDtypeStruct(gram.shape, F32),
        compiler_params=pltpu.CompilerParams(vmem_limit_bytes=VMEM_LIMIT),
        cost_estimate=cost(2**32, 2**22),
    )(gram)


def solve_kernel(parts_ref, inverse_ref, out_ref):
    total = jnp.sum(parts_ref[...].astype(F32), axis=0)
    out_ref[...] = jnp.dot(inverse_ref[...], total, precision=HIGH, preferred_element_type=F32).astype(BF16)


def solve_right(parts, inverse):
    return pl.pallas_call(
        solve_kernel,
        out_shape=jax.ShapeDtypeStruct(parts.shape[1:], BF16),
        compiler_params=pltpu.CompilerParams(vmem_limit_bytes=VMEM_LIMIT),
        cost_estimate=cost(0, 0),
    )(parts, inverse)


def touch_kernel(acts_ref, out_ref):
    out_ref[...] = acts_ref[: out_ref.shape[0], : out_ref.shape[1]]


def touch(res_acts):
    vmem = pl.BlockSpec(memory_space=pltpu.VMEM)
    return pl.pallas_call(
        touch_kernel,
        in_specs=[vmem],
        out_specs=vmem,
        out_shape=jax.ShapeDtypeStruct((16, 128), res_acts.dtype),
        compiler_params=pltpu.CompilerParams(vmem_limit_bytes=VMEM_LIMIT),
        cost_estimate=cost(0, 2 * res_acts.size),
    )(res_acts)


def left_kernel(acts_ref, token_ref, *refs):
    refs[-1][...] = contract_last(acts_ref[...], stack_rows(refs[:-1]))


def on_left(sketches, res_acts, token):
    rows, tokens = len(sketches) * sketches[0].shape[1], res_acts.shape[0]
    return pl.pallas_call(
        left_kernel,
        in_specs=[pl.BlockSpec(memory_space=pltpu.VMEM)] * (2 + len(sketches)),
        out_specs=pl.BlockSpec(memory_space=pltpu.VMEM),
        out_shape=jax.ShapeDtypeStruct((tokens, rows), F32),
        compiler_params=pltpu.CompilerParams(vmem_limit_bytes=VMEM_LIMIT),
        cost_estimate=cost(0, 0),
    )(res_acts, token, *sketches)


def sum_ranks(product, first, queries, rank):
    shape = (product.shape[1], queries)
    chosen = lax.broadcasted_iota(jnp.int32, shape, 0) // rank + first == lax.broadcasted_iota(jnp.int32, shape, 1)
    chosen = chosen.astype(F32).astype(BF16)
    total = 0.0
    for _ in range(2):
        term = product.astype(BF16)
        total = total + jnp.dot(term, chosen, preferred_element_type=F32)
        product = product - term.astype(F32)
    return total


def make_score_kernel(score_scale, wide, high):
    def score_kernel(place_ref, own_ref, other_ref, grads_ref, *refs):
        rights, out_ref = refs[:-1], refs[-1]
        queries = out_ref.shape[0]
        half, rank = queries // 2, rights[0].shape[1]
        place = place_ref[0]
        core, row, column = place % 2, place // 2 % high, place // (2 * high)
        chips = [(column + wide - x) % wide * high + (row + high - y) % high for x, y in STEPS]
        order = [2 * chip + core for chip in chips] + [2 * chip + 1 - core for chip in chips]
        total = 0.0
        for j, left_ref in enumerate((own_ref, other_ref)):
            right = jnp.concatenate([ref[i] for ref in rights for i in range(j, ref.shape[0], 2)], axis=0)
            product = left_ref[...] * contract_last(grads_ref[...], right)
            total = total + sum_ranks(product, j * half, queries, rank)
        sums = total.T * score_scale
        for i, query in enumerate(order):
            out_ref[pl.ds(query, 1), :] = sums[i : i + 1]

    return score_kernel


def all_scores(place, own, other, rights, res_grads, score_scale, sizes):
    queries = sum(x.shape[0] for x in rights)
    vmem = pl.BlockSpec(memory_space=pltpu.VMEM)
    return pl.pallas_call(
        make_score_kernel(score_scale, *sizes),
        in_specs=[pl.BlockSpec(memory_space=pltpu.SMEM)] + [vmem] * (3 + len(rights)),
        out_specs=vmem,
        out_shape=jax.ShapeDtypeStruct((queries, own.shape[0]), F32),
        compiler_params=pltpu.CompilerParams(vmem_limit_bytes=VMEM_LIMIT),
        cost_estimate=cost(2 * own.size * res_grads.shape[1], 2 * res_grads.size),
    )(place, own, other, res_grads, *rights)


def from_back(block, axis, step):
    size = lax.axis_size(axis)
    return lax.ppermute(block, axis, [(i, (i + step) % size) for i in range(size)])


STEPS = ((0, 0), (1, 0), (0, 1), (1, 1), (0, 3), (1, 3), (0, 2), (1, 2))


def local(query_acts, query_grads, sketch_maps, res_acts, res_grads):
    rank, outs = sketch_maps.shape[1:]
    groups = lax.axis_size(TOK)
    score_scale = 1.0 / math.sqrt(rank * outs * query_acts.shape[1] * groups)

    place = lax.axis_index(QUERY).astype(jnp.int32).reshape(1)
    partial = partial_sketch(sketch_maps, query_grads, query_acts, groups)
    partial, place = lax.optimization_barrier((partial, place))
    parts = exchange(partial, TOK)
    sketch = exchange(sum_pieces(parts), TOK)
    right_part, gram = partial_right(sketch, query_acts, query_grads)
    sketch, right_part = lax.optimization_barrier((sketch, right_part))
    right_parts = exchange(right_part, TOK)

    inverse = invert(gram)
    right = solve_right(right_parts, inverse)

    beside, behind, ahead = from_back(sketch, "xlo", 1), from_back(sketch, "y", 1), from_back(sketch, "y", 3)
    _, beside, behind = lax.optimization_barrier((inverse, beside, behind))
    corners = [from_back(beside, "y", 1), from_back(beside, "y", 3)]
    across = [from_back(behind, "y", 1), from_back(corners[1], "y", 3)]
    right, ahead = lax.optimization_barrier((right, ahead))
    both = jnp.stack([right, swap_cores(right)])
    early = [sketch, beside, behind, corners[0], ahead, corners[1], across[0]]
    both, acts, *early = lax.optimization_barrier((both, res_acts, *early))
    both = jnp.concatenate([both, from_back(both, "xlo", 1)])
    other_early = [swap_cores(block) for block in early]
    both, token = lax.optimization_barrier((both, touch(acts)))
    rights = [both] + [from_back(both, "y", step) for step in (1, 3, 2)]
    token, last, *early = lax.optimization_barrier((token, across[1], *early))
    own_left = on_left(early + [last], acts, token)
    other_left = on_left(other_early + [swap_cores(last)], acts, token)
    sizes = lax.axis_size("xlo"), lax.axis_size("y")
    return all_scores(place, own_left, other_left, rights, res_grads, score_scale, sizes)


def solution(mesh):
    fine = Mesh(mesh.devices.reshape(2, 4, 2, 8, 2), QUERY + TOK)
    in_specs = (
        P(QUERY, TOK, None),
        P(QUERY, TOK, None),
        P(QUERY, None, None),
        P(QUERY + TOK, None),
        P(QUERY + TOK, None),
    )
    return jax.shard_map(local, mesh=fine, in_specs=in_specs, out_specs=P(None, QUERY + TOK), check_vma=False)
```
